32 devices in a mesh: freq: 2 (over x), row: 2 (over y), col: 8 (over z, core).
Axes of the slice: x: 2, y: 2, z: 4, core: 2. Of those that a mesh axis runs over, the one named last changes fastest.
Arguments:
- eps_slab: bfloat16 [4096, 30720], P(('freq', 'row'), 'col'), parts along dimension 0, may hold values from -0.03125 to 0.03125
- matrix_elements: bfloat16 [512, 30720], P('col'), may hold values from -6 to 6
- band_energy: float32 [512], replicated, may hold values from -2 to 2
- frequency: float32 [2], P('freq'), parts along dimension 0, may hold values from -1 to 1
Outputs:
- sigma: float32 [1024, 512], P(('freq', 'col'), 'row'), parts along dimension 0
The draws below stay inside these ranges and needn't reach their ends.
There are 2 independent parts, one for each index of `freq`. The reference program is written for one: setup_inputs(seed, part) draws one part's arguments, and reference() takes and returns one part's arrays. A program takes and returns all parts, laid end to end along the dimension named above; an argument that names none is the same for every part. Nothing has to cross between parts.
All inputs are finite; a program needn't handle non-finite values.
Results may differ from the reference program's by a relative error of at most 0.0003.
Values may be sent and summed in bfloat16 or wider, within the bound.
A program may use at most 64 MiB of HBM per device.

```python
import math
import jax
import jax.numpy as jnp
from jax import lax

NPW = 30720
ROWS_DEV = 1024
ROWS = 2048
PAIRS = 512
N_ROW = 2


def level_of(own_key, extent, shards, least, largest):
    loudness, own = 1.0, jax.random.fold_in(own_key, 6)
    for position, blocks in shards:
        heights = jnp.exp(jax.random.uniform(jax.random.fold_in(own, position), (blocks,), jnp.float32, least / len(shards), largest / len(shards)))
        loudness = loudness * jnp.repeat(heights, extent[position] // blocks).reshape([-1 if axis == position else 1 for axis in range(len(extent))])
    return loudness


def bell_draw(own_key, extent, deviation, reach, cuts=(), held_as=jnp.bfloat16):
    loudness = level_of(own_key, extent, cuts, -0.22, 0.18) if cuts else 1.0
    entries = jax.random.normal(own_key, extent, jnp.float32) * deviation * loudness
    return jnp.minimum(jnp.maximum(entries, -reach), reach).astype(held_as)


def setup_inputs(seed: int = 0, part: int = 0) -> dict:
    key_list = jax.random.split(jax.random.key(seed), 5)
    part_keys = jax.random.split(jax.random.fold_in(key_list[4], part), 5)
    eps_slab = bell_draw(part_keys[0], (ROWS, NPW), NPW ** -0.5, 0.03125, ((0, 2), (1, 8)))
    matrix_elements = bell_draw(key_list[1], (PAIRS, NPW), 1.0, 6.0, ((0, 8),))
    band_energy = jnp.clip(jax.random.uniform(key_list[2], (PAIRS,), jnp.float32, -2.0, 2.0), -2.0, 2.0)
    frequency = jnp.clip(jax.random.uniform(part_keys[3], (1,), jnp.float32, -1.0, 1.0), -1.0, 1.0)
    return {"eps_slab": eps_slab, "matrix_elements": matrix_elements, "band_energy": band_energy, "frequency": frequency}


def reference(eps_slab, matrix_elements, band_energy, frequency):
    elements = matrix_elements.astype(jnp.float32)
    blocks = eps_slab.reshape(N_ROW, ROWS_DEV, NPW)

    def block_product(block):
        return lax.dot_general(block.astype(jnp.float32), elements, (((1,), (1,)), ((), ())), precision=lax.Precision.HIGHEST, preferred_element_type=jnp.float32)
    screened = lax.map(block_product, blocks).reshape(ROWS, PAIRS)
    weight = 1.0 / (1.0 + (frequency[0] - band_energy) ** 2)
    weighted = elements[:, :ROWS] * weight[:, None]
    sigma = lax.dot_general(screened, weighted, (((0,), (1,)), ((), ())), precision=lax.Precision.HIGHEST, preferred_element_type=jnp.float32)
    return sigma * (1.0 / math.sqrt(ROWS))
```

```python
import functools
import math

import jax
import jax.numpy as jnp
from jax import lax
from jax.experimental import pallas as pl
from jax.experimental.pallas import tpu as pltpu
from jax.sharding import PartitionSpec as P

MESH = pl.DeviceIdType.MESH
F32 = jnp.float32
BF16 = jnp.bfloat16


def flip(index, mask):
    bit = 1
    while bit <= mask:
        if mask & bit:
            index = index + bit * (1 - 2 * lax.rem(index // bit, 2))
        bit *= 2
    return index


def kernel(
    dims,
    eps_hbm, m_hbm, band_ref, freq_ref, out_ref,
    eps_v, slab, mbuf, thi, tlo, part, sib, qsum, yrecv, rsum, zrecv,
    local_sem, slab_send, slab_recv, m_send, m_recv,
    sib_send, sib_recv, y_send, y_recv, z_send, z_recv,
):
    n_row, n_col, rows, width, pw = dims
    n_chip = n_col // 2
    pairs = n_col * pw
    quarter = pw // 4
    n_half = pairs // n_row
    left_cols = -(-width // 256) * 128
    right_cols = width - left_cols

    f = lax.axis_index("freq")
    r = lax.axis_index("row")
    c = lax.axis_index("col")
    o = lax.rem(c, 2)
    parity = lax.rem(r, 2)
    xf = 1 - f
    yr = r + 1 - 2 * parity
    me = (f, r, c)
    x_dev = (xf, r, c)
    y_dev = (f, yr, c)
    sib_dev = (f, r, flip(c, 1))

    def rows_of(panel, first, count):
        return pl.ds(pl.multiple_of(panel * pw + first, 16), count)

    def cols_of(index, size):
        return pl.ds(pl.multiple_of(index * size, 128), size)

    load_eps = pltpu.make_async_copy(eps_hbm, eps_v, local_sem.at[0])
    load_eps.start()
    load_slab = pltpu.make_async_copy(
        m_hbm.at[:, cols_of(r, rows)], slab.at[rows_of(c, 0, pw)], local_sem.at[1])
    load_slab.start()
    load_m = pltpu.make_async_copy(
        m_hbm.at[:, cols_of(c, width)], mbuf.at[rows_of(c, 0, pw)], local_sem.at[2])
    load_m.start()

    barrier = pltpu.get_barrier_semaphore()
    for d in range(1, n_col):
        pl.semaphore_signal(barrier, inc=1, device_id=(f, r, flip(c, d)), device_id_type=MESH)
    pl.semaphore_signal(barrier, inc=1, device_id=x_dev, device_id_type=MESH)
    for dr in range(1, n_row):
        pl.semaphore_signal(barrier, inc=1, device_id=(f, lax.rem(r + dr, n_row), c), device_id_type=MESH)
    pl.semaphore_wait(barrier, n_col - 1 + 1 + n_row - 1)

    def copy(src, dst, send, recv, device):
        return pltpu.make_async_remote_copy(
            src_ref=src, dst_ref=dst, send_sem=send, recv_sem=recv,
            device_id=device, device_id_type=MESH)

    pending = []

    def start(desc):
        desc.start()
        pending.append(desc)

    def arrived(dst, recv):
        copy(dst, dst, recv, recv, me).wait_recv()

    chip_order = list(range(1, n_chip))
    remote = [2 * dk + dc for dk in chip_order for dc in range(2)]

    start(copy(m_hbm.at[:, cols_of(r, rows)], slab.at[rows_of(c, 0, pw)],
               slab_send.at[0, 1], slab_recv.at[0, 1], sib_dev))
    for d in remote:
        to = flip(c, d)
        q = quarter * (2 * f + lax.rem(to, 2))
        start(copy(m_hbm.at[pl.ds(pl.multiple_of(q, 16), quarter), cols_of(r, rows)],
                   slab.at[rows_of(c, q, quarter)],
                   slab_send.at[0, d], slab_recv.at[0, d], (f, r, to)))
    start(copy(m_hbm.at[:, cols_of(flip(c, 1), width)], mbuf.at[rows_of(c, 0, pw)],
               m_send.at[0, 1], m_recv.at[0, 1], sib_dev))
    mq = quarter * (2 * f + parity)
    mq_x = quarter * (2 * xf + parity)
    mq_y = quarter * (2 * f + 1 - parity)
    mq_d = quarter * (2 * xf + 1 - parity)
    for d in remote:
        to = flip(c, d)
        start(copy(m_hbm.at[pl.ds(pl.multiple_of(mq, 16), quarter), cols_of(to, width)],
                   mbuf.at[rows_of(c, mq, quarter)],
                   m_send.at[0, d], m_recv.at[0, d], (f, r, to)))

    sq = quarter * (2 * f + o)
    sq_x = quarter * (2 * xf + o)
    sq_s = quarter * (2 * f + 1 - o)
    sq_d = quarter * (2 * xf + 1 - o)
    for d in remote:
        own = slab.at[rows_of(flip(c, d), sq, quarter)]
        arrived(own, slab_recv.at[0, d])
        start(copy(own, own, slab_send.at[1, d], slab_recv.at[1, d], x_dev))
        start(copy(own, own, slab_send.at[2, d], slab_recv.at[2, d ^ 1], sib_dev))
    for d in remote:
        got = slab.at[rows_of(flip(c, d), sq_x, quarter)]
        arrived(got, slab_recv.at[1, d])
        start(copy(got, got, slab_send.at[3, d], slab_recv.at[3, d ^ 1], sib_dev))
    load_slab.wait()
    arrived(slab.at[rows_of(flip(c, 1), 0, pw)], slab_recv.at[0, 1])
    for d in remote:
        panel = flip(c, d)
        arrived(slab.at[rows_of(panel, sq_s, quarter)], slab_recv.at[2, d])
        arrived(slab.at[rows_of(panel, sq_d, quarter)], slab_recv.at[3, d])
    load_eps.wait()

    t_cols = 256 if width % 256 == 0 else 128
    t_steps = width // t_cols

    def t_range(first, last):
        @pl.loop(first, last)
        def _(step):
            cols = cols_of(step, t_cols)
            t = jnp.dot(slab[...], eps_v[:, cols], preferred_element_type=F32)
            hi = t.astype(BF16)
            thi[:, cols] = hi
            tlo[:, cols] = (t - hi.astype(F32)).astype(BF16)

    lcols = pl.ds(0, left_cols)
    rcols = pl.ds(left_cols, right_cols)

    def forward_first(dk):
        for d in (2 * dk, 2 * dk + 1):
            own = mbuf.at[rows_of(flip(c, d), mq, quarter)]
            arrived(own, m_recv.at[0, d])
            start(copy(own, own, m_send.at[1, d], m_recv.at[1, d], x_dev))
            start(copy(own, own, m_send.at[2, d], m_recv.at[2, d], y_dev))

    def forward_second(dk):
        for d in (2 * dk, 2 * dk + 1):
            from_x = mbuf.at[rows_of(flip(c, d), mq_x, quarter)]
            from_y = mbuf.at[rows_of(flip(c, d), mq_y, quarter)]
            arrived(from_x, m_recv.at[1, d])
            half = from_x.at[:, lcols]
            start(copy(half, half, m_send.at[3, d], m_recv.at[3, d], y_dev))
            arrived(from_y, m_recv.at[2, d])
            half = from_y.at[:, rcols]
            start(copy(half, half, m_send.at[4, d], m_recv.at[4, d], x_dev))

    k_cols = width // 5 if width % 640 == 0 else 128
    k_steps = width // k_cols

    def product(dk):
        for d in (2 * dk, 2 * dk + 1):
            panel = flip(c, d)
            if d == 0:
                load_m.wait()
            elif d == 1:
                arrived(mbuf.at[rows_of(panel, 0, pw)], m_recv.at[0, 1])
            else:
                diag = mbuf.at[rows_of(panel, mq_d, quarter)]
                arrived(diag.at[:, lcols], m_recv.at[3, d])
                arrived(diag.at[:, rcols], m_recv.at[4, d])
        chip_rows = pl.ds(pl.multiple_of(flip(c, 2 * dk) // 2 * (2 * pw), 2 * pw), 2 * pw)
        part[dk] = jnp.zeros((2 * pw, pairs), F32)

        @pl.loop(0, k_steps)
        def _(step):
            cols = cols_of(step, k_cols)
            m = mbuf[chip_rows, cols]
            nt = (((1,), (1,)), ((), ()))
            part[dk] += (
                lax.dot_general(m, thi[:, cols], nt, preferred_element_type=F32)
                + lax.dot_general(m, tlo[:, cols], nt, preferred_element_type=F32))

        theirs = part.at[dk, pl.ds(pl.multiple_of((1 - o) * pw, pw), pw)]
        start(copy(theirs, sib.at[dk], sib_send.at[dk], sib_recv.at[dk], sib_dev))

    def add_sibling(dk):
        arrived(sib.at[dk], sib_recv.at[dk])
        qsum[dk] = part[dk, pl.ds(pl.multiple_of(o * pw, pw), pw)] + sib[dk]
        for dr in range(1, n_row):
            to = lax.rem(r + dr, n_row)
            start(copy(qsum.at[dk, :, cols_of(to, n_half)], yrecv.at[dk, dr - 1],
                       y_send.at[dk, dr - 1], y_recv.at[dk, dr - 1], (f, to, c)))

    def add_rows(dk):
        total = qsum[dk, :, cols_of(r, n_half)]
        for dr in range(1, n_row):
            arrived(yrecv.at[dk, dr - 1], y_recv.at[dk, dr - 1])
            total += yrecv[dk, dr - 1]
        rsum[dk] = total
        if dk:
            start(copy(rsum.at[dk], zrecv.at[dk], z_send.at[dk], z_recv.at[dk],
                       (f, r, flip(c, 2 * dk))))

    first = chip_order[0]
    third = t_steps // 3
    t_range(0, third)
    forward_first(first)
    t_range(third, 2 * third)
    forward_second(first)
    t_range(2 * third, t_steps)
    done = 0
    product(0)
    for dk in chip_order[1:]:
        forward_first(dk)
        add_sibling(done)
        forward_second(dk)
        add_rows(done)
        done = chip_order[chip_order.index(dk) - 1]
        product(done)
    add_sibling(done)
    last = chip_order[-1]
    if last != done:
        add_rows(done)
        product(last)
        add_sibling(last)
    add_rows(last)

    total = rsum[0]
    for dk in chip_order:
        arrived(zrecv.at[dk], z_recv.at[dk])
        total += zrecv[dk]
    band = band_ref[:, cols_of(r, n_half)]
    weight = 1.0 / (1.0 + (freq_ref[0] - band) ** 2)
    out_ref[...] = total * (weight * (1.0 / math.sqrt(rows * n_row)))
    for desc in pending:
        desc.wait_send()


def shards(eps_slab, matrix_elements, band_energy, frequency):
    rows, width = eps_slab.shape
    pw = matrix_elements.shape[0]
    n_col = lax.axis_size("col")
    n_row = lax.axis_size("row")
    n_chip = n_col // 2
    pairs = pw * n_col
    n_half = pairs // n_row
    dma = pltpu.SemaphoreType.DMA
    hbm = pl.BlockSpec(memory_space=pl.ANY)
    return pl.pallas_call(
        functools.partial(kernel, (n_row, n_col, rows, width, pw)),
        out_shape=jax.ShapeDtypeStruct((pw, n_half), F32),
        in_specs=[hbm, hbm, pl.BlockSpec(memory_space=pltpu.VMEM), pl.BlockSpec(memory_space=pltpu.SMEM)],
        out_specs=pl.BlockSpec(memory_space=pltpu.VMEM),
        scratch_shapes=[
            pltpu.VMEM((rows, width), BF16),
            pltpu.VMEM((pairs, rows), BF16),
            pltpu.VMEM((pairs, width), BF16),
            pltpu.VMEM((pairs, width), BF16),
            pltpu.VMEM((pairs, width), BF16),
            pltpu.VMEM((n_chip, 2 * pw, pairs), F32),
            pltpu.VMEM((n_chip, pw, pairs), F32),
            pltpu.VMEM((n_chip, pw, pairs), F32),
            pltpu.VMEM((n_chip, n_row - 1, pw, n_half), F32),
            pltpu.VMEM((n_chip, pw, n_half), F32),
            pltpu.VMEM((n_chip, pw, n_half), F32),
            dma((3,)),
            dma((4, n_col)), dma((4, n_col)),
            dma((5, n_col)), dma((5, n_col)),
            dma((n_chip,)), dma((n_chip,)),
            dma((n_chip, n_row - 1)), dma((n_chip, n_row - 1)),
            dma((n_chip,)), dma((n_chip,)),
        ],
        compiler_params=pltpu.CompilerParams(
            collective_id=0, has_side_effects=True, vmem_limit_bytes=56 * 2 ** 20),
        cost_estimate=pl.CostEstimate(
            flops=2 * pairs * width * (rows + 2 * pairs),
            bytes_accessed=2 * rows * width + 2 * pw * width * n_col, transcendentals=0),
    )(eps_slab, matrix_elements, band_energy.reshape(1, pairs), frequency)


def solution(mesh):
    in_specs = (P(("freq", "row"), "col"), P("col", None), P(), P("freq"))
    out_specs = P(("freq", "col"), "row")
    return jax.shard_map(shards, mesh=mesh, in_specs=in_specs, out_specs=out_specs, check_vma=False)
```

```python
import functools
import math

import jax
import jax.numpy as jnp
from jax import lax
from jax.experimental import pallas as pl
from jax.experimental.pallas import tpu as pltpu
from jax.sharding import PartitionSpec as P

MESH = pl.DeviceIdType.MESH
F32 = jnp.float32
BF16 = jnp.bfloat16


def flip(index, mask):
    bit = 1
    while bit <= mask:
        if mask & bit:
            index = index + bit * (1 - 2 * lax.rem(index // bit, 2))
        bit *= 2
    return index


def kernel(
    dims,
    eps_hbm, m_hbm, band_ref, freq_ref, out_ref,
    eps_v, slab, mbuf, thi, tlo, part, sib, qsum, yrecv, rsum, zrecv,
    local_sem, slab_send, slab_recv, m_send, m_recv,
    sib_send, sib_recv, y_send, y_recv, z_send, z_recv,
):
    n_row, n_col, rows, width, pw, stages = dims
    n_chip = n_col // 2
    pairs = n_col * pw
    quarter = pw // 4
    n_half = pairs // n_row

    f = lax.axis_index("freq")
    r = lax.axis_index("row")
    c = lax.axis_index("col")
    o = lax.rem(c, 2)
    parity = lax.rem(r, 2)
    xf = 1 - f
    yr = r + 1 - 2 * parity
    me = (f, r, c)
    x_dev = (xf, r, c)
    y_dev = (f, yr, c)
    sib_dev = (f, r, flip(c, 1))

    def rows_of(panel, first, count):
        return pl.ds(pl.multiple_of(panel * pw + first, 16), count)

    def cols_of(index, size):
        return pl.ds(pl.multiple_of(index * size, 128), size)

    load_eps = pltpu.make_async_copy(eps_hbm, eps_v, local_sem.at[0])
    load_eps.start()
    load_slab = pltpu.make_async_copy(
        m_hbm.at[:, cols_of(r, rows)], slab.at[rows_of(c, 0, pw)], local_sem.at[1])
    load_slab.start()
    load_m = pltpu.make_async_copy(
        m_hbm.at[:, cols_of(c, width)], mbuf.at[rows_of(c, 0, pw)], local_sem.at[2])
    load_m.start()

    barrier = pltpu.get_barrier_semaphore()
    for d in range(1, n_col):
        pl.semaphore_signal(barrier, inc=1, device_id=(f, r, flip(c, d)), device_id_type=MESH)
    pl.semaphore_signal(barrier, inc=1, device_id=x_dev, device_id_type=MESH)
    for dr in range(1, n_row):
        pl.semaphore_signal(barrier, inc=1, device_id=(f, lax.rem(r + dr, n_row), c), device_id_type=MESH)
    pl.semaphore_wait(barrier, n_col - 1 + 1 + n_row - 1)

    def copy(src, dst, send, recv, device):
        return pltpu.make_async_remote_copy(
            src_ref=src, dst_ref=dst, send_sem=send, recv_sem=recv,
            device_id=device, device_id_type=MESH)

    pending = []

    def start(desc):
        desc.start()
        pending.append(desc)

    def arrived(dst, recv):
        copy(dst, dst, recv, recv, me).wait_recv()

    far_first = list(range(n_chip - 1, 0, -1))
    remote = [2 * dk + dc for dk in far_first for dc in range(2)]
    k_cols = width // stages
    t_cols = 256 if k_cols % 256 == 0 else 128

    start(copy(m_hbm.at[:, cols_of(r, rows)], slab.at[rows_of(c, 0, pw)],
               slab_send.at[0, 1], slab_recv.at[0, 1], sib_dev))
    for d in remote:
        to = flip(c, d)
        q = quarter * (2 * f + lax.rem(to, 2))
        start(copy(m_hbm.at[pl.ds(pl.multiple_of(q, 16), quarter), cols_of(r, rows)],
                   slab.at[rows_of(c, q, quarter)],
                   slab_send.at[0, d], slab_recv.at[0, d], (f, r, to)))

    mq = quarter * (2 * f + parity)
    mq_x = quarter * (2 * xf + parity)
    mq_y = quarter * (2 * f + 1 - parity)
    mq_d = quarter * (2 * xf + 1 - parity)

    def block(panel, first, stage):
        return mbuf.at[rows_of(panel, first, quarter), pl.ds(stage * k_cols, k_cols)]

    def send_z(stage, d):
        to = flip(c, d)
        cols = pl.ds(pl.multiple_of(to * width + stage * k_cols, 128), k_cols)
        start(copy(m_hbm.at[pl.ds(pl.multiple_of(mq, 16), quarter), cols], block(c, mq, stage),
                   m_send.at[0, stage, d], m_recv.at[0, stage, d], (f, r, to)))

    def forward_first(stage):
        for d in remote:
            own = block(flip(c, d), mq, stage)
            arrived(own, m_recv.at[0, stage, d])
            start(copy(own, own, m_send.at[1, stage, d], m_recv.at[1, stage, d], x_dev))
            start(copy(own, own, m_send.at[2, stage, d], m_recv.at[2, stage, d], y_dev))
            if stage + 2 < stages:
                send_z(stage + 2, d)

    def forward_second(stage):
        for d in remote:
            panel = flip(c, d)
            from_x, from_y = block(panel, mq_x, stage), block(panel, mq_y, stage)
            arrived(from_x, m_recv.at[1, stage, d])
            arrived(from_y, m_recv.at[2, stage, d])
            if d % 2 == 0:
                start(copy(from_x, from_x, m_send.at[3, stage, d], m_recv.at[3, stage, d], y_dev))
            else:
                start(copy(from_y, from_y, m_send.at[3, stage, d], m_recv.at[3, stage, d], x_dev))

    def t_chunk(stage):
        @pl.loop(0, k_cols // t_cols)
        def _(step):
            cols = pl.ds(pl.multiple_of(stage * k_cols + step * t_cols, 128), t_cols)
            t = jnp.dot(slab[...], eps_v[:, cols], preferred_element_type=F32)
            hi = t.astype(BF16)
            thi[:, cols] = hi
            tlo[:, cols] = (t - hi.astype(F32)).astype(BF16)

    def wait_chunk(stage):
        for d in remote:
            arrived(block(flip(c, d), mq_d, stage), m_recv.at[3, stage, d])
        if stage == 0:
            load_m.wait()
            arrived(mbuf.at[rows_of(flip(c, 1), 0, pw)], m_recv.at[0, 0, 1])

    n_cols = 256 if pairs % 256 == 0 else 128

    def product(stage, m_rows):
        cols = pl.ds(stage * k_cols, k_cols)
        nt = (((1,), (1,)), ((), ()))

        @pl.loop(0, pairs // n_cols)
        def _(step):
            ns = pl.ds(pl.multiple_of(step * n_cols, n_cols), n_cols)
            m = mbuf[m_rows, cols]
            p = (lax.dot_general(m, thi[ns, cols], nt, preferred_element_type=F32)
                 + lax.dot_general(m, tlo[ns, cols], nt, preferred_element_type=F32))
            out_cols = pl.ds(pl.multiple_of(step * n_cols, n_cols), n_cols)
            if stage:
                part[m_rows, out_cols] += p
            else:
                part[m_rows, out_cols] = p

    def panel_rows(dk, core):
        return rows_of(2 * (flip(c, 2 * dk) // 2) + core, 0, pw)

    def send_sibling(dk):
        start(copy(part.at[panel_rows(dk, 1 - o)], sib.at[dk], sib_send.at[dk], sib_recv.at[dk], sib_dev))

    def add_sibling(dk):
        arrived(sib.at[dk], sib_recv.at[dk])
        qsum[dk] = part[panel_rows(dk, o), :] + sib[dk]
        for dr in range(1, n_row):
            to = lax.rem(r + dr, n_row)
            start(copy(qsum.at[dk, :, cols_of(to, n_half)], yrecv.at[dk, dr - 1],
                       y_send.at[dk, dr - 1], y_recv.at[dk, dr - 1], (f, to, c)))

    def add_rows(dk):
        total = qsum[dk, :, cols_of(r, n_half)]
        for dr in range(1, n_row):
            arrived(yrecv.at[dk, dr - 1], y_recv.at[dk, dr - 1])
            total += yrecv[dk, dr - 1]
        rsum[dk] = total
        if dk:
            start(copy(rsum.at[dk], zrecv.at[dk], z_send.at[dk], z_recv.at[dk],
                       (f, r, flip(c, 2 * dk))))

    for stage in range(min(2, stages)):
        for d in remote:
            send_z(stage, d)
    start(copy(m_hbm.at[:, cols_of(flip(c, 1), width)], mbuf.at[rows_of(c, 0, pw)],
               m_send.at[0, 0, 1], m_recv.at[0, 0, 1], sib_dev))

    sq = quarter * (2 * f + o)
    sq_x = quarter * (2 * xf + o)
    sq_s = quarter * (2 * f + 1 - o)
    sq_d = quarter * (2 * xf + 1 - o)
    for d in remote:
        own = slab.at[rows_of(flip(c, d), sq, quarter)]
        arrived(own, slab_recv.at[0, d])
        start(copy(own, own, slab_send.at[1, d], slab_recv.at[1, d], x_dev))
        start(copy(own, own, slab_send.at[2, d], slab_recv.at[2, d ^ 1], sib_dev))
    forward_first(0)
    for d in remote:
        got = slab.at[rows_of(flip(c, d), sq_x, quarter)]
        arrived(got, slab_recv.at[1, d])
        start(copy(got, got, slab_send.at[3, d], slab_recv.at[3, d ^ 1], sib_dev))
    forward_second(0)
    if stages > 1:
        forward_first(1)
    load_slab.wait()
    arrived(slab.at[rows_of(flip(c, 1), 0, pw)], slab_recv.at[0, 1])
    for d in remote:
        panel = flip(c, d)
        arrived(slab.at[rows_of(panel, sq_s, quarter)], slab_recv.at[2, d])
        arrived(slab.at[rows_of(panel, sq_d, quarter)], slab_recv.at[3, d])
    load_eps.wait()
    t_chunk(0)
    all_rows = pl.ds(0, pairs)
    for stage in range(stages - 1):
        forward_second(stage + 1)
        if stage + 2 < stages:
            forward_first(stage + 2)
        t_chunk(stage + 1)
        wait_chunk(stage)
        product(stage, all_rows)

    wait_chunk(stages - 1)
    order = far_first + [0]
    for i, dk in enumerate(order):
        product(stages - 1, rows_of(2 * (flip(c, 2 * dk) // 2), 0, 2 * pw))
        send_sibling(dk)
        if i >= 1:
            add_sibling(order[i - 1])
        if i >= 2:
            add_rows(order[i - 2])
    add_sibling(order[-1])
    for dk in order[-2:]:
        add_rows(dk)

    total = rsum[0]
    for dk in far_first:
        arrived(zrecv.at[dk], z_recv.at[dk])
        total += zrecv[dk]
    band = band_ref[:, cols_of(r, n_half)]
    weight = 1.0 / (1.0 + (freq_ref[0] - band) ** 2)
    out_ref[...] = total * (weight * (1.0 / math.sqrt(rows * n_row)))
    for desc in pending:
        desc.wait_send()


def shards(eps_slab, matrix_elements, band_energy, frequency):
    rows, width = eps_slab.shape
    pw = matrix_elements.shape[0]
    n_col = lax.axis_size("col")
    n_row = lax.axis_size("row")
    n_chip = n_col // 2
    pairs = pw * n_col
    n_half = pairs // n_row
    stages = next(n for n in (5, 4, 3, 2, 1) if width % (128 * n) == 0)
    dma = pltpu.SemaphoreType.DMA
    hbm = pl.BlockSpec(memory_space=pl.ANY)
    return pl.pallas_call(
        functools.partial(kernel, (n_row, n_col, rows, width, pw, stages)),
        out_shape=jax.ShapeDtypeStruct((pw, n_half), F32),
        in_specs=[hbm, hbm, pl.BlockSpec(memory_space=pltpu.VMEM), pl.BlockSpec(memory_space=pltpu.SMEM)],
        out_specs=pl.BlockSpec(memory_space=pltpu.VMEM),
        scratch_shapes=[
            pltpu.VMEM((rows, width), BF16),
            pltpu.VMEM((pairs, rows), BF16),
            pltpu.VMEM((pairs, width), BF16),
            pltpu.VMEM((pairs, width), BF16),
            pltpu.VMEM((pairs, width), BF16),
            pltpu.VMEM((pairs, pairs), F32),
            pltpu.VMEM((n_chip, pw, pairs), F32),
            pltpu.VMEM((n_chip, pw, pairs), F32),
            pltpu.VMEM((n_chip, n_row - 1, pw, n_half), F32),
            pltpu.VMEM((n_chip, pw, n_half), F32),
            pltpu.VMEM((n_chip, pw, n_half), F32),
            dma((3,)),
            dma((4, n_col)), dma((4, n_col)),
            dma((4, stages, n_col)), dma((4, stages, n_col)),
            dma((n_chip,)), dma((n_chip,)),
            dma((n_chip, n_row - 1)), dma((n_chip, n_row - 1)),
            dma((n_chip,)), dma((n_chip,)),
        ],
        compiler_params=pltpu.CompilerParams(
            collective_id=0, has_side_effects=True, vmem_limit_bytes=56 * 2 ** 20),
        cost_estimate=pl.CostEstimate(
            flops=2 * pairs * width * (rows + 2 * pairs),
            bytes_accessed=2 * rows * width + 2 * pw * width * n_col, transcendentals=0),
    )(eps_slab, matrix_elements, band_energy.reshape(1, pairs), frequency)


def solution(mesh):
    in_specs = (P(("freq", "row"), "col"), P("col", None), P(), P("freq"))
    out_specs = P(("freq", "col"), "row")
    return jax.shard_map(shards, mesh=mesh, in_specs=in_specs, out_specs=out_specs, check_vma=False)
```

```python
import functools
import math

import jax
import jax.numpy as jnp
from jax import lax
from jax.experimental import pallas as pl
from jax.experimental.pallas import tpu as pltpu
from jax.sharding import PartitionSpec as P

MESH = pl.DeviceIdType.MESH
F32 = jnp.float32
BF16 = jnp.bfloat16


def flip(index, mask):
    bit = 1
    while bit <= mask:
        if mask & bit:
            index = index + bit * (1 - 2 * lax.rem(index // bit, 2))
        bit *= 2
    return index


def kernel(
    dims,
    eps_hbm, m_hbm, band_ref, freq_ref, out_ref,
    eps_v, slab, mbuf, thi, tlo, part, sib, qsum, yrecv, rsum, zrecv,
    local_sem, slab_send, slab_recv, m_send, m_recv,
    sib_send, sib_recv, y_send, y_recv, z_send, z_recv,
):
    n_row, n_col, rows, width, pw, stages = dims
    n_chip = n_col // 2
    pairs = n_col * pw
    quarter = pw // 4
    n_half = pairs // n_row

    f = lax.axis_index("freq")
    r = lax.axis_index("row")
    c = lax.axis_index("col")
    o = lax.rem(c, 2)
    parity = lax.rem(r, 2)
    xf = 1 - f
    yr = r + 1 - 2 * parity
    me = (f, r, c)
    x_dev = (xf, r, c)
    y_dev = (f, yr, c)
    sib_dev = (f, r, flip(c, 1))

    def rows_of(panel, first, count):
        return pl.ds(pl.multiple_of(panel * pw + first, 16), count)

    def cols_of(index, size):
        return pl.ds(pl.multiple_of(index * size, 128), size)

    load_eps = pltpu.make_async_copy(eps_hbm, eps_v, local_sem.at[0])
    load_eps.start()
    load_slab = pltpu.make_async_copy(
        m_hbm.at[:, cols_of(r, rows)], slab.at[rows_of(c, 0, pw)], local_sem.at[1])
    load_slab.start()
    load_m = pltpu.make_async_copy(
        m_hbm.at[:, cols_of(c, width)], mbuf.at[rows_of(c, 0, pw)], local_sem.at[2])
    load_m.start()

    barrier = pltpu.get_barrier_semaphore()
    for d in range(1, n_col):
        pl.semaphore_signal(barrier, inc=1, device_id=(f, r, flip(c, d)), device_id_type=MESH)
    pl.semaphore_signal(barrier, inc=1, device_id=x_dev, device_id_type=MESH)
    for dr in range(1, n_row):
        pl.semaphore_signal(barrier, inc=1, device_id=(f, lax.rem(r + dr, n_row), c), device_id_type=MESH)
    pl.semaphore_wait(barrier, n_col - 1 + 1 + n_row - 1)

    def copy(src, dst, send, recv, device):
        return pltpu.make_async_remote_copy(
            src_ref=src, dst_ref=dst, send_sem=send, recv_sem=recv,
            device_id=device, device_id_type=MESH)

    pending = []

    def start(desc):
        desc.start()
        pending.append(desc)

    def arrived(dst, recv):
        copy(dst, dst, recv, recv, me).wait_recv()

    far_first = list(range(n_chip - 1, 0, -1))
    remote = [2 * dk + dc for dk in far_first for dc in range(2)]
    k_cols = width // stages
    t_cols = 256 if k_cols % 256 == 0 else 128

    start(copy(m_hbm.at[:, cols_of(r, rows)], slab.at[rows_of(c, 0, pw)],
               slab_send.at[0, 1], slab_recv.at[0, 1], sib_dev))
    for d in remote:
        to = flip(c, d)
        q = quarter * (2 * f + lax.rem(to, 2))
        start(copy(m_hbm.at[pl.ds(pl.multiple_of(q, 16), quarter), cols_of(r, rows)],
                   slab.at[rows_of(c, q, quarter)],
                   slab_send.at[0, d], slab_recv.at[0, d], (f, r, to)))

    mq = quarter * (2 * f + parity)
    mq_x = quarter * (2 * xf + parity)
    mq_y = quarter * (2 * f + 1 - parity)
    mq_d = quarter * (2 * xf + 1 - parity)

    def block(panel, first, stage):
        return mbuf.at[rows_of(panel, first, quarter), pl.ds(stage * k_cols, k_cols)]

    def send_z(stage, d):
        to = flip(c, d)
        cols = pl.ds(pl.multiple_of(to * width + stage * k_cols, 128), k_cols)
        start(copy(m_hbm.at[pl.ds(pl.multiple_of(mq, 16), quarter), cols], block(c, mq, stage),
                   m_send.at[0, stage, d], m_recv.at[0, stage, d], (f, r, to)))

    def forward_first(stage):
        for d in remote:
            own = block(flip(c, d), mq, stage)
            arrived(own, m_recv.at[0, stage, d])
            start(copy(own, own, m_send.at[1, stage, d], m_recv.at[1, stage, d], x_dev))
            start(copy(own, own, m_send.at[2, stage, d], m_recv.at[2, stage, d], y_dev))
            if stage + 2 < stages:
                send_z(stage + 2, d)

    def forward_second(stage):
        for d in remote:
            panel = flip(c, d)
            from_x, from_y = block(panel, mq_x, stage), block(panel, mq_y, stage)
            if d % 2 == 0:
                arrived(from_x, m_recv.at[1, stage, d])
                start(copy(from_x, from_x, m_send.at[3, stage, d], m_recv.at[3, stage, d], y_dev))
            else:
                arrived(from_y, m_recv.at[2, stage, d])
                start(copy(from_y, from_y, m_send.at[3, stage, d], m_recv.at[3, stage, d], x_dev))

    def t_chunk(stage):
        @pl.loop(0, k_cols // t_cols)
        def _(step):
            cols = pl.ds(pl.multiple_of(stage * k_cols + step * t_cols, 128), t_cols)
            t = jnp.dot(slab[...], eps_v[:, cols], preferred_element_type=F32)
            hi = t.astype(BF16)
            thi[:, cols] = hi
            tlo[:, cols] = (t - hi.astype(F32)).astype(BF16)

    def wait_chunk(stage):
        for d in remote:
            panel = flip(c, d)
            if d % 2 == 0:
                arrived(block(panel, mq_y, stage), m_recv.at[2, stage, d])
            else:
                arrived(block(panel, mq_x, stage), m_recv.at[1, stage, d])
            arrived(block(panel, mq_d, stage), m_recv.at[3, stage, d])
        if stage == 0:
            load_m.wait()
            arrived(mbuf.at[rows_of(flip(c, 1), 0, pw)], m_recv.at[0, 0, 1])

    n_cols = 256 if pairs % 256 == 0 else 128

    def product(stage, m_rows):
        cols = pl.ds(stage * k_cols, k_cols)
        nt = (((1,), (1,)), ((), ()))

        @pl.loop(0, pairs // n_cols)
        def _(step):
            ns = pl.ds(pl.multiple_of(step * n_cols, n_cols), n_cols)
            m = mbuf[m_rows, cols]
            p = (lax.dot_general(m, thi[ns, cols], nt, preferred_element_type=F32)
                 + lax.dot_general(m, tlo[ns, cols], nt, preferred_element_type=F32))
            out_cols = pl.ds(pl.multiple_of(step * n_cols, n_cols), n_cols)
            if stage:
                part[m_rows, out_cols] += p
            else:
                part[m_rows, out_cols] = p

    def panel_rows(dk, core):
        return rows_of(2 * (flip(c, 2 * dk) // 2) + core, 0, pw)

    def send_sibling(dk):
        start(copy(part.at[panel_rows(dk, 1 - o)], sib.at[dk], sib_send.at[dk], sib_recv.at[dk], sib_dev))

    def add_sibling(dk):
        arrived(sib.at[dk], sib_recv.at[dk])
        qsum[dk] = part[panel_rows(dk, o), :] + sib[dk]
        for dr in range(1, n_row):
            to = lax.rem(r + dr, n_row)
            start(copy(qsum.at[dk, :, cols_of(to, n_half)], yrecv.at[dk, dr - 1],
                       y_send.at[dk, dr - 1], y_recv.at[dk, dr - 1], (f, to, c)))

    def add_rows(dk):
        total = qsum[dk, :, cols_of(r, n_half)]
        for dr in range(1, n_row):
            arrived(yrecv.at[dk, dr - 1], y_recv.at[dk, dr - 1])
            total += yrecv[dk, dr - 1]
        rsum[dk] = total
        if dk:
            start(copy(rsum.at[dk], zrecv.at[dk], z_send.at[dk], z_recv.at[dk],
                       (f, r, flip(c, 2 * dk))))

    for stage in range(min(2, stages)):
        for d in remote:
            send_z(stage, d)
    start(copy(m_hbm.at[:, cols_of(flip(c, 1), width)], mbuf.at[rows_of(c, 0, pw)],
               m_send.at[0, 0, 1], m_recv.at[0, 0, 1], sib_dev))

    sq = quarter * (2 * f + o)
    sq_x = quarter * (2 * xf + o)
    sq_s = quarter * (2 * f + 1 - o)
    sq_d = quarter * (2 * xf + 1 - o)
    for d in remote:
        own = slab.at[rows_of(flip(c, d), sq, quarter)]
        arrived(own, slab_recv.at[0, d])
        start(copy(own, own, slab_send.at[1, d], slab_recv.at[1, d], x_dev))
        start(copy(own, own, slab_send.at[2, d], slab_recv.at[2, d ^ 1], sib_dev))
    forward_first(0)
    for d in remote:
        got = slab.at[rows_of(flip(c, d), sq_x, quarter)]
        arrived(got, slab_recv.at[1, d])
        start(copy(got, got, slab_send.at[3, d], slab_recv.at[3, d ^ 1], sib_dev))
    if stages > 1:
        forward_first(1)
    forward_second(0)
    load_slab.wait()
    arrived(slab.at[rows_of(flip(c, 1), 0, pw)], slab_recv.at[0, 1])
    for d in remote:
        panel = flip(c, d)
        arrived(slab.at[rows_of(panel, sq_s, quarter)], slab_recv.at[2, d])
        arrived(slab.at[rows_of(panel, sq_d, quarter)], slab_recv.at[3, d])
    load_eps.wait()
    t_chunk(0)
    all_rows = pl.ds(0, pairs)
    for stage in range(stages - 1):
        if stage + 2 < stages:
            forward_first(stage + 2)
        forward_second(stage + 1)
        t_chunk(stage + 1)
        wait_chunk(stage)
        product(stage, all_rows)

    wait_chunk(stages - 1)
    order = far_first + [0]
    for i, dk in enumerate(order):
        product(stages - 1, rows_of(2 * (flip(c, 2 * dk) // 2), 0, 2 * pw))
        send_sibling(dk)
        if i >= 1:
            add_sibling(order[i - 1])
        if i >= 2:
            add_rows(order[i - 2])
    add_sibling(order[-1])
    for dk in order[-2:]:
        add_rows(dk)

    total = rsum[0]
    for dk in far_first:
        arrived(zrecv.at[dk], z_recv.at[dk])
        total += zrecv[dk]
    band = band_ref[:, cols_of(r, n_half)]
    weight = 1.0 / (1.0 + (freq_ref[0] - band) ** 2)
    out_ref[...] = total * (weight * (1.0 / math.sqrt(rows * n_row)))
    for desc in pending:
        desc.wait_send()


def shards(eps_slab, matrix_elements, band_energy, frequency):
    rows, width = eps_slab.shape
    pw = matrix_elements.shape[0]
    n_col = lax.axis_size("col")
    n_row = lax.axis_size("row")
    n_chip = n_col // 2
    pairs = pw * n_col
    n_half = pairs // n_row
    stages = next(n for n in (5, 4, 3, 2, 1) if width % (128 * n) == 0)
    dma = pltpu.SemaphoreType.DMA
    hbm = pl.BlockSpec(memory_space=pl.ANY)
    return pl.pallas_call(
        functools.partial(kernel, (n_row, n_col, rows, width, pw, stages)),
        out_shape=jax.ShapeDtypeStruct((pw, n_half), F32),
        in_specs=[hbm, hbm, pl.BlockSpec(memory_space=pltpu.VMEM), pl.BlockSpec(memory_space=pltpu.SMEM)],
        out_specs=pl.BlockSpec(memory_space=pltpu.VMEM),
        scratch_shapes=[
            pltpu.VMEM((rows, width), BF16),
            pltpu.VMEM((pairs, rows), BF16),
            pltpu.VMEM((pairs, width), BF16),
            pltpu.VMEM((pairs, width), BF16),
            pltpu.VMEM((pairs, width), BF16),
            pltpu.VMEM((pairs, pairs), F32),
            pltpu.VMEM((n_chip, pw, pairs), F32),
            pltpu.VMEM((n_chip, pw, pairs), F32),
            pltpu.VMEM((n_chip, n_row - 1, pw, n_half), F32),
            pltpu.VMEM((n_chip, pw, n_half), F32),
            pltpu.VMEM((n_chip, pw, n_half), F32),
            dma((3,)),
            dma((4, n_col)), dma((4, n_col)),
            dma((4, stages, n_col)), dma((4, stages, n_col)),
            dma((n_chip,)), dma((n_chip,)),
            dma((n_chip, n_row - 1)), dma((n_chip, n_row - 1)),
            dma((n_chip,)), dma((n_chip,)),
        ],
        compiler_params=pltpu.CompilerParams(
            collective_id=0, has_side_effects=True, vmem_limit_bytes=56 * 2 ** 20),
        cost_estimate=pl.CostEstimate(
            flops=2 * pairs * width * (rows + 2 * pairs),
            bytes_accessed=2 * rows * width + 2 * pw * width * n_col, transcendentals=0),
    )(eps_slab, matrix_elements, band_energy.reshape(1, pairs), frequency)


def solution(mesh):
    in_specs = (P(("freq", "row"), "col"), P("col", None), P(), P("freq"))
    out_specs = P(("freq", "col"), "row")
    return jax.shard_map(shards, mesh=mesh, in_specs=in_specs, out_specs=out_specs, check_vma=False)
```
